32 devices in a mesh: stn: 4 (over y, x), tm: 8 (over z, core).
Axes of the slice: x: 2, y: 2, z: 4, core: 2. Of those that a mesh axis runs over, the one named last changes fastest.
Arguments:
- voltages: bfloat16 [512, 128, 4096], P('stn', 'tm'), may hold values from -52 to 52
- pfb_taps: float32 [16, 4096], replicated, may hold values from -1.5 to 1.5
- eq_gains: float32 [512, 2048], P('stn'), may hold values from 0.5 to 11
Outputs:
- visibilities: float32 [2048, 512, 512], P(('stn', 'tm'))
The draws below stay inside these ranges and needn't reach their ends.
All inputs are finite; a program needn't handle non-finite values.
Results may differ from the reference program's by a relative error of at most 0.0014.
Values may be sent and summed in bfloat16 or wider, within the bound.
A program may use at most 448 MiB of HBM per device.

```python
import math
import jax
import jax.numpy as jnp
from jax import lax

CHANNELS = 2048
TAPS = 16
INPUTS = 512
FRAMES = 128
FFT_LEN = 4096


def draw_voltages(key, part):
    keys = jax.random.split(key, 4)
    shape = (INPUTS, FRAMES, FFT_LEN)
    position = jnp.arange(FRAMES, dtype=jnp.float32) / (FRAMES - 1)
    coupling = jax.random.uniform(keys[2], (INPUTS, 1, 1), jnp.float32, 0.2, 1.0)
    roughness = jnp.exp(jax.random.uniform(keys[3], (INPUTS, FRAMES, 1), jnp.float32, math.log(0.5), math.log(2.0)))
    noise = jnp.clip(jax.random.normal(keys[0], shape, jnp.float32), -4.0, 4.0)
    common = jnp.clip(jax.random.normal(keys[1], (1, FRAMES, FFT_LEN), jnp.float32), -4.0, 4.0)
    drift = jnp.exp(0.5 * math.log(10.0) * position)
    return ((noise + coupling * common) * roughness * drift[None, :, None]).astype(jnp.bfloat16)


def draw_eq_gains(key, part):
    channel_pos = jnp.arange(CHANNELS, dtype=jnp.float32) / (CHANNELS - 1)
    rough_gain = jnp.exp(jax.random.uniform(key, (INPUTS, CHANNELS), jnp.float32, math.log(0.5), math.log(2.0)))
    bandpass = jnp.exp(0.5 * math.log(10.0) * channel_pos)
    return rough_gain * bandpass[None, :]


def bell_draw(stream_key, dims, spread, bound, kind=jnp.bfloat16):
    array = spread * jax.random.normal(stream_key, dims, jnp.float32)
    return jnp.clip(array, min=-bound, max=bound).astype(kind)


def setup_inputs(seed: int = 0) -> dict:
    arg_keys = jax.random.split(jax.random.key(seed), 4)
    voltages = draw_voltages(jax.random.fold_in(arg_keys[3], 71), 0)
    pfb_taps = bell_draw(arg_keys[1], (TAPS, FFT_LEN), TAPS ** -0.5, 1.5, jnp.float32)
    eq_gains = draw_eq_gains(jax.random.fold_in(arg_keys[3], 71), 0)
    return {"voltages": voltages, "pfb_taps": pfb_taps, "eq_gains": eq_gains}


chan_block = 8

def channelize(volt_row, gain_row, pfb_taps):
    frames = volt_row.astype(jnp.float32)
    history_len = TAPS - 1
    padded = jnp.concatenate([jnp.zeros((history_len, FFT_LEN), jnp.float32), frames], axis=0)
    filtered = jnp.zeros((FRAMES, FFT_LEN), jnp.float32)
    for tap_index in range(TAPS):
        first_row = history_len - tap_index
        filtered = filtered + pfb_taps[tap_index][None, :] * padded[first_row:first_row + FRAMES]
    spectrum = jnp.fft.rfft(filtered, axis=-1)[:, :CHANNELS]
    spec_re = (jnp.real(spectrum) * gain_row[None, :]).astype(jnp.bfloat16)
    spec_im = (jnp.imag(spectrum) * gain_row[None, :]).astype(jnp.bfloat16)
    return (spec_re, spec_im)

def reference(voltages, pfb_taps, eq_gains):
    spec_re, spec_im = lax.map(lambda pair: channelize(pair[0], pair[1], pfb_taps), (voltages, eq_gains))
    power = lax.optimization_barrier(jnp.sum(jnp.square(spec_re.astype(jnp.float32)) + jnp.square(spec_im.astype(jnp.float32)), axis=(1, 2)))
    scale = lax.rsqrt(power / (FRAMES * CHANNELS) + 1e-06)
    weight = scale[:, None] * scale[None, :] / FRAMES
    row_ids = lax.broadcasted_iota(jnp.int32, (INPUTS, INPUTS), 0)
    col_ids = lax.broadcasted_iota(jnp.int32, (INPUTS, INPUTS), 1)
    lower = row_ids >= col_ids
    re_blocks = jnp.transpose(spec_re, (2, 0, 1)).reshape(CHANNELS // chan_block, chan_block, INPUTS, FRAMES)
    im_blocks = jnp.transpose(spec_im, (2, 0, 1)).reshape(CHANNELS // chan_block, chan_block, INPUTS, FRAMES)
    highest = lax.Precision.HIGHEST

    def correlate(pair):
        part_re = pair[0].astype(jnp.float32)
        part_im = pair[1].astype(jnp.float32)
        vis_re = jnp.einsum('cat,cbt->cab', part_re, part_re, precision=highest) + jnp.einsum('cat,cbt->cab', part_im, part_im, precision=highest)
        vis_im = jnp.einsum('cat,cbt->cab', part_im, part_re, precision=highest) - jnp.einsum('cat,cbt->cab', part_re, part_im, precision=highest)
        return jnp.where(lower[None], vis_re, vis_im) * weight[None]
    packed = lax.map(correlate, (re_blocks, im_blocks))
    return packed.reshape(CHANNELS, INPUTS, INPUTS)
```

```python
import functools
import math

import jax
import jax.numpy as jnp
import ml_dtypes
import numpy as np
from jax import lax
from jax.experimental import pallas as pl
from jax.experimental.pallas import tpu as pltpu
from jax.sharding import PartitionSpec as P


def from_behind(value, axis, steps):
    count = lax.axis_size(axis)
    first, last = (max(0, -steps), min(count, count - steps))
    return lax.ppermute(value, axis, [(source, source + steps) for source in range(first, last)])


def cos_sin(numer, denom):
    angle = 2.0 * math.pi / denom * (numer % denom).astype(jnp.float32)
    return (jnp.cos(angle), jnp.sin(angle))


def transform(filtered, channels):
    inputs_dev, frames_dev, length = filtered.shape
    inner_len = 64
    outer_len = length // inner_len
    kept_upper = channels // outer_len
    row_count = inputs_dev * frames_dev
    highest = lax.Precision.HIGHEST
    arranged = filtered.reshape(row_count, outer_len, inner_len)
    freq_one = lax.broadcasted_iota(jnp.int32, (outer_len, outer_len), 0)
    time_one = lax.broadcasted_iota(jnp.int32, (outer_len, outer_len), 1)
    cos_one, sin_one = cos_sin(freq_one * time_one, outer_len)
    section_one = jnp.stack([cos_one, -sin_one])
    partial_ft = jnp.einsum("qka,Rab->qkbR", section_one, arranged, precision=highest)
    freq_twist = lax.broadcasted_iota(jnp.int32, (outer_len, inner_len), 0)
    time_twist = lax.broadcasted_iota(jnp.int32, (outer_len, inner_len), 1)
    twist_cos, twist_sin = cos_sin(freq_twist * time_twist, length)
    twist_table = jnp.stack([jnp.stack([twist_cos, twist_sin]), jnp.stack([-twist_sin, twist_cos])])
    freq_two = lax.broadcasted_iota(jnp.int32, (kept_upper, inner_len), 0)
    time_two = lax.broadcasted_iota(jnp.int32, (kept_upper, inner_len), 1)
    cos_two, sin_two = cos_sin(freq_two * time_two, inner_len)
    section_two = jnp.stack(
        [jnp.stack([cos_two, sin_two], axis=1), jnp.stack([-sin_two, cos_two], axis=1)]
    )
    combined = jnp.einsum("qjrb,rskb->qjksb", section_two, twist_table, precision=highest)
    spectrum = jnp.einsum("qjksb,skbR->qjkR", combined, partial_ft, precision=highest)
    return spectrum.reshape(2, channels, row_count)


def per_device(voltages, pfb_taps, eq_gains):
    tap_count = pfb_taps.shape[0]
    history_len = tap_count - 1
    inputs_dev, frames_dev, length = voltages.shape
    channels = eq_gains.shape[1]
    station_groups = lax.axis_size("stn")
    time_groups = lax.axis_size("tm")
    per_group = channels // (station_groups * time_groups)
    all_inputs = inputs_dev * station_groups
    all_frames = frames_dev * time_groups
    earlier = from_behind(voltages[:, frames_dev - history_len :, :], "tm", 1)
    extended = jnp.concatenate([earlier, voltages], axis=1).astype(jnp.float32)
    kernel = jnp.flip(pfb_taps, axis=0)[:, None, :]
    filtered = lax.conv_general_dilated(
        extended,
        kernel,
        (1,),
        "VALID",
        dimension_numbers=("NWC", "WIO", "NWC"),
        feature_group_count=length,
        precision=lax.Precision.HIGHEST,
    )
    spectrum = transform(filtered, channels)
    gains_turned = jnp.transpose(eq_gains)
    spectra = (
        spectrum.reshape(2, channels, inputs_dev, frames_dev) * gains_turned[None, :, :, None]
    ).astype(jnp.bfloat16)
    shaped = spectra.reshape(2, station_groups * time_groups, per_group, inputs_dev * frames_dev)
    turned = lax.all_to_all(shaped, ("stn", "tm"), split_axis=1, concat_axis=1, tiled=True)
    blocks = turned.reshape(2, station_groups, time_groups, per_group, inputs_dev, frames_dev)
    columns = jnp.transpose(blocks, (0, 3, 1, 4, 2, 5)).reshape(
        2, per_group, all_inputs, all_frames
    )
    swapped = jnp.stack([columns[1], -columns[0]])
    vis_real = jnp.einsum("rcnt,rcmt->cnm", columns, columns, preferred_element_type=jnp.float32)
    vis_imag = jnp.einsum("rcnt,rcmt->cnm", swapped, columns, preferred_element_type=jnp.float32)
    local_power = jnp.sum(jnp.diagonal(vis_real, axis1=1, axis2=2), axis=0)
    power = lax.psum(local_power, ("stn", "tm"))
    scale = lax.rsqrt(power / (all_frames * channels) + 1e-06)
    weight = scale[:, None] * scale[None, :] / all_frames
    row_ids = lax.broadcasted_iota(jnp.int32, (all_inputs, all_inputs), 0)
    col_ids = lax.broadcasted_iota(jnp.int32, (all_inputs, all_inputs), 1)
    lower = row_ids >= col_ids
    return jnp.where(lower[None], vis_real, vis_imag) * weight[None]


OUTER = 16
INNER = 256
NT = (((1,), (1,)), ((), ()))
TN = (((0,), (0,)), ((), ()))


def split_pair(table):
    high = table.astype(ml_dtypes.bfloat16)
    low = (table - high.astype(np.float64)).astype(ml_dtypes.bfloat16)
    return np.stack([high, low])


def dft_tables(length):
    def parts(residue):
        freq = residue + OUTER * np.arange(INNER // 2)[:, None]
        angle = -2.0 * np.pi / length * ((freq * np.arange(INNER)[None, :]) % length)
        return np.cos(angle), np.sin(angle)

    pairs = []
    for residue in range(1, OUTER // 2):
        c, s = parts(residue)
        cm, sm = parts(OUTER - residue)
        pairs.append(np.block([[c, -s], [s, c], [cm, sm], [sm, -cm]]))
    singles = [np.concatenate(parts(residue)) for residue in (0, OUTER // 2)]
    return split_pair(np.stack(pairs)), split_pair(np.stack(singles))


def real_dft16(x):
    r = math.sqrt(0.5)
    s = [x[n] + x[n + 8] for n in range(8)]
    d = [x[n] - x[n + 8] for n in range(8)]
    t = [s[n] + s[n + 4] for n in range(4)]
    u = [s[n] - s[n + 4] for n in range(4)]
    even, odd = t[0] + t[2], t[1] + t[3]
    minus, plus = (u[1] - u[3]) * r, (u[1] + u[3]) * r
    out = {
        0: (even + odd, None),
        8: (even - odd, None),
        4: (t[0] - t[2], t[3] - t[1]),
        2: (u[0] + minus, -plus - u[2]),
        6: (u[0] - minus, u[2] - plus),
    }
    e = [None] + [d[n] - d[8 - n] for n in range(1, 4)]
    g = [None] + [d[n] + d[8 - n] for n in range(1, 4)]
    for k in (1, 3, 5, 7):
        re, im = d[0], d[4] * (-math.sin(math.pi * k / 2))
        for n in range(1, 4):
            re = re + e[n] * math.cos(math.pi * n * k / 8)
            im = im - g[n] * math.sin(math.pi * n * k / 8)
        out[k] = (re, im)
    return out


def channelize_kernel(
    first, x_ref, taps_ref, gain_ref, pair_ref, single_ref, out_ref, power_ref, y_hi, y_lo, spec
):
    step = pl.program_id(0)
    tap_count = taps_ref.shape[0]
    inputs = x_ref.shape[1]
    groups, per_group = out_ref.shape[0], out_ref.shape[3]
    row_tiles = inputs // 16

    def filter_rows(index, carry):
        frame = index // row_tiles
        tile = index % row_tiles
        rows = pl.ds(pl.multiple_of(tile * 16, 16), 16)
        out_rows = pl.ds(pl.multiple_of(index * 16, 16), 16)
        base = first + 2 * step + frame + tap_count - 1
        for half in range(INNER // 128):
            values = []
            for block in range(OUTER):
                lanes = pl.ds(block * INNER + half * 128, 128)
                total = None
                for tap in range(tap_count):
                    sample = x_ref[base - tap, rows, lanes].astype(jnp.float32)
                    term = sample.reshape(2, 8, 128) * taps_ref[tap, :, lanes]
                    total = term if total is None else total + term
                values.append(total.reshape(16, 128))
            for k, both in real_dft16(values).items():
                for part, value in enumerate(both):
                    if value is None:
                        continue
                    slot = {0: 0, 8: 1}.get(k, 2 * k) + part
                    lanes = pl.ds(slot * INNER + half * 128, 128)
                    high = value.astype(jnp.bfloat16)
                    y_hi[out_rows, lanes] = high
                    y_lo[out_rows, lanes] = (value - high.astype(jnp.float32)).astype(jnp.bfloat16)
        return carry

    lax.fori_loop(0, 2 * row_tiles, filter_rows, 0)

    def product(table, index, lanes):
        high, low = y_hi[:, lanes], y_lo[:, lanes]
        dot = functools.partial(
            lax.dot_general, dimension_numbers=NT, preferred_element_type=jnp.float32
        )
        return dot(table[0, index], high) + (dot(table[1, index], high) + dot(table[0, index], low))

    def spread(result, row, residue):
        for part in range(2):
            for frame in range(2):
                first_row = row + part * (INNER // 2)
                spec[2 * part + frame, pl.ds(residue, INNER // 2, stride=OUTER), :] = result[
                    first_row : first_row + INNER // 2, frame * inputs : (frame + 1) * inputs
                ]

    for residue in range(1, OUTER // 2):
        result = product(pair_ref, residue - 1, pl.ds(2 * residue * INNER, 2 * INNER))
        spread(result, 0, residue)
        spread(result, INNER, OUTER - residue)
    for index, residue in enumerate((0, OUTER // 2)):
        spread(product(single_ref, index, pl.ds(index * INNER, INNER)), 0, residue)

    def finish(group, power):
        rows = pl.ds(pl.multiple_of(group * per_group, per_group), per_group)
        gain = gain_ref[rows, :]
        for part in range(2):
            for frame in range(2):
                rounded = (spec[2 * part + frame, rows, :] * gain).astype(jnp.bfloat16)
                out_ref[group, frame, part] = rounded
                wide = rounded.astype(jnp.float32)
                power = power + jnp.sum((wide * wide).reshape(per_group // 8, 8, inputs), axis=0)
        return power

    power_ref[0] = lax.fori_loop(0, groups, finish, jnp.zeros((8, inputs), jnp.float32))


def channelize(extended, taps, gains, tables, first, frames, groups):
    inputs, length = extended.shape[1:]
    channels = gains.shape[0]
    per_group = channels // groups
    steps = frames // 2
    whole = lambda array: pl.BlockSpec(
        array.shape, lambda i: (0,) * array.ndim, pipeline_mode=pl.Buffered(1)
    )
    return pl.pallas_call(
        functools.partial(channelize_kernel, first),
        grid=(steps,),
        in_specs=[whole(array) for array in (extended, taps, gains, *tables)],
        out_specs=[
            pl.BlockSpec((groups, 2, 2, per_group, inputs), lambda i: (0, i, 0, 0, 0)),
            pl.BlockSpec((1, 8, inputs), lambda i: (i, 0, 0)),
        ],
        out_shape=[
            jax.ShapeDtypeStruct((groups, frames, 2, per_group, inputs), jnp.bfloat16),
            jax.ShapeDtypeStruct((steps, 8, inputs), jnp.float32),
        ],
        scratch_shapes=[
            pltpu.VMEM((2 * inputs, length), jnp.bfloat16),
            pltpu.VMEM((2 * inputs, length), jnp.bfloat16),
            pltpu.VMEM((4, channels, inputs), jnp.float32),
        ],
        compiler_params=pltpu.CompilerParams(vmem_limit_bytes=62 * 2**20),
        cost_estimate=pl.CostEstimate(
            flops=frames * inputs * channels * 12000, bytes_accessed=60 * 2**20, transcendentals=0
        ),
        name="channelize",
    )(extended, taps, gains, *tables)


def correlate_kernel(stations, *refs):
    *part_refs, weight_ref, out_ref, columns = refs
    sub = pl.program_id(1)
    sub_count = out_ref.shape[0]
    half_frames = columns.shape[1] // 2
    inputs = columns.shape[2]

    @pl.when(sub == 0)
    def _():
        row = 0
        for ref in part_refs:
            times = ref.shape[0] // stations
            frames, _, _, lanes = ref.shape[1:]

            def turn(index, carry, ref=ref, row=row, times=times, frames=frames, lanes=lanes):
                for station in range(stations):
                    for part in range(2):
                        block = ref[station * times + index, :, part].astype(jnp.float32)
                        start = part * half_frames + row + index * frames
                        columns[
                            :,
                            pl.ds(pl.multiple_of(start, 8), frames),
                            station * lanes : (station + 1) * lanes,
                        ] = jnp.transpose(block, (1, 0, 2))
                return carry

            lax.fori_loop(0, times, turn, 0)
            row += times * frames

    half = inputs // 2
    dot = functools.partial(
        lax.dot_general, dimension_numbers=TN, preferred_element_type=jnp.float32
    )
    lower = lax.broadcasted_iota(jnp.int32, (half, half), 0) >= lax.broadcasted_iota(
        jnp.int32, (half, half), 1
    )

    def one(index, carry):
        straight = columns[sub * sub_count + index].astype(jnp.bfloat16)
        turned = jnp.concatenate([straight[half_frames:], -straight[:half_frames]], axis=0)
        for row in range(2):
            for col in range(2):
                rows = slice(row * half, (row + 1) * half)
                cols = slice(col * half, (col + 1) * half)
                right = straight[:, cols]
                if row > col:
                    value = dot(straight[:, rows], right)
                elif row < col:
                    value = dot(turned[:, rows], right)
                else:
                    value = jnp.where(
                        lower, dot(straight[:, rows], right), dot(turned[:, rows], right)
                    )
                out_ref[index, rows, cols] = value * weight_ref[rows, cols]
        return carry

    lax.fori_loop(0, sub_count, one, 0)


def correlate(parts, weight, stations):
    devices, _, _, per_group, lanes = parts[0].shape
    inputs = stations * lanes
    all_frames = sum(part.shape[1] for part in parts) * (devices // stations)
    tile, sub = 16, 4
    return pl.pallas_call(
        functools.partial(correlate_kernel, stations),
        grid=(per_group // tile, tile // sub),
        in_specs=[
            pl.BlockSpec((devices, part.shape[1], 2, tile, lanes), lambda i, j: (0, 0, 0, i, 0))
            for part in parts
        ]
        + [pl.BlockSpec((inputs, inputs), lambda i, j: (0, 0))],
        out_specs=pl.BlockSpec((sub, inputs, inputs), lambda i, j: (i * (tile // sub) + j, 0, 0)),
        out_shape=jax.ShapeDtypeStruct((per_group, inputs, inputs), jnp.float32),
        scratch_shapes=[pltpu.VMEM((tile, 2 * all_frames, inputs), jnp.float32)],
        compiler_params=pltpu.CompilerParams(vmem_limit_bytes=56 * 2**20),
        name="correlate",
    )(*parts, weight)


def per_device_tiled(voltages, pfb_taps, eq_gains):
    tap_count, length = pfb_taps.shape
    history_len = tap_count - 1
    inputs_dev, frames_dev, _ = voltages.shape
    channels = eq_gains.shape[1]
    station_groups = lax.axis_size("stn")
    time_groups = lax.axis_size("tm")
    groups = station_groups * time_groups
    all_inputs = inputs_dev * station_groups
    all_frames = frames_dev * time_groups
    frame_major = jnp.transpose(voltages, (1, 0, 2))
    earlier = from_behind(frame_major[frames_dev - history_len :], "tm", 1)
    extended = jnp.concatenate([earlier, frame_major], axis=0)
    taps = jnp.broadcast_to(pfb_taps[:, None, :], (tap_count, 8, length))
    gains = jnp.transpose(eq_gains)
    tables = [jnp.asarray(table) for table in dft_tables(length)]
    piece = frames_dev // PIECES
    received, power = [], 0.0
    for index in range(PIECES):
        spectra, partial = channelize(
            extended, taps, gains, tables, index * piece, piece, groups
        )
        received.append(
            lax.all_to_all(spectra, ("stn", "tm"), split_axis=0, concat_axis=0, tiled=True)
        )
        power = power + jnp.sum(partial, axis=(0, 1))
    placed = lax.dynamic_update_slice(
        jnp.zeros((all_inputs,), jnp.float32), power, (lax.axis_index("stn") * inputs_dev,)
    )
    power = lax.psum(placed, ("stn", "tm"))
    scale = lax.rsqrt(power / (all_frames * channels) + 1e-06)
    weight = scale[:, None] * scale[None, :] / all_frames
    return correlate(received, weight, station_groups)


PIECES = 2


def fits_tiles(mesh, voltages, pfb_taps, eq_gains):
    inputs = voltages.shape[0] // mesh.shape["stn"]
    frames = voltages.shape[1] // mesh.shape["tm"]
    per_group = eq_gains.shape[1] // mesh.size
    return (
        voltages.shape[2] == OUTER * INNER
        and 2 * eq_gains.shape[1] == voltages.shape[2]
        and inputs == 128
        and frames == 16
        and pfb_taps.shape[0] == 16
        and per_group % 16 == 0
        and voltages.shape[:2] == (512, 128)
    )


def solution(mesh):
    in_specs = (P("stn", "tm", None), P(), P("stn", None))
    out_specs = P(("stn", "tm"), None, None)

    def run(voltages, pfb_taps, eq_gains):
        body = per_device_tiled if fits_tiles(mesh, voltages, pfb_taps, eq_gains) else per_device
        return jax.shard_map(
            body, mesh=mesh, in_specs=in_specs, out_specs=out_specs, check_vma=False
        )(voltages, pfb_taps, eq_gains)

    return run
```
